256 devices in a mesh: gx: 32 (over x_hi, z, core), gy: 8 (over y, x_lo).
Axes of the slice: x: 4 (x_hi: 2, x_lo: 2; x = x_hi * 2 + x_lo), y: 4, z: 8, core: 2. Of those that a mesh axis runs over, the one named last changes fastest.
Arguments:
- rhs: float32 [32, 8, 4, 320], P('gx', 'gy'), may hold values from -120 to 120
- vol_jac: float32 [32, 8, 4, 320, 320], P('gx', 'gy'), may hold values from -0.3125 to 0.3125
- inv_step: float32 [32, 8, 4], P('gx', 'gy'), may hold values from 4 to 16
- face_jac: float32 [32, 8, 4, 6, 5, 5], P('gx', 'gy'), may hold values from -1 to 1
- orientation: int32 [32, 8, 4, 6], P('gx', 'gy'), may hold values from 0 to 7, as said below
Outputs:
- newton_update: float32 [32, 8, 4, 320], P('gx', 'gy')
- residual_ratio: float32 [], replicated
The draws below stay inside these ranges and needn't reach their ends.
Inputs may be any that keep to these rules, and one draw needn't show every extreme that they name: `orientation`: the two sides of every face carry inverse codes: where one side has code o, the other has o if o < 4, else 4 + (o & 2) / 2 + 2 (o & 1).
All inputs are finite; a program needn't handle non-finite values.
Results may differ from the reference program's by a relative error of at most 0.0025.
Values sent between devices are 32-bit elements; how exact they have to be, the bound alone decides.
No kernel may reach another device: no remote copies, remote signals or barrier semaphores. Data moves between devices by JAX's collectives and lax.ppermute only.
A program may use at most 256 MiB of HBM per device.

```python
import math
import jax
import jax.numpy as jnp
import numpy as np
from jax import lax

Q = 4
NV = 5
ITERS = 3
NS_STEPS = 3
NP = 64
BLK = 320
NX = 32
NY = 8
NZ = 4


def draw_rhs(key, part):
    noise_key, scale_key = jax.random.split(jax.random.fold_in(key, 11))
    full_shape = (NX, NY, NZ, BLK)
    ramp_first = jnp.arange(NX, dtype=jnp.float32)[:, None, None, None]
    ramp_second = jnp.arange(NY, dtype=jnp.float32)[None, :, None, None]
    position_ramp = 1.0 + 2.0 * (ramp_first + ramp_second) / (NX + NY - 2)
    noise_part = jax.random.truncated_normal(noise_key, -4.0, 4.0, full_shape, jnp.float32)
    spread = 10.0 ** jax.random.uniform(scale_key, (NX, NY, NZ, 1), jnp.float32, 0.0, 1.0)
    return noise_part * spread * position_ramp


def inverse_code(codes):
    swapped = 4 + codes // 2 % 2 + 2 * (codes % 2)
    return jnp.where(codes >= 4, swapped, codes)


def draw_orientation(key, part):
    upper_codes = jax.random.randint(jax.random.fold_in(key, 23), (NX, NY, NZ, 3), 0, 8, dtype=jnp.int32)
    sides = []
    for direction_id in range(3):
        upper_side = upper_codes[..., direction_id]
        lower_side = inverse_code(jnp.roll(upper_side, 1, axis=direction_id))
        sides.append(lower_side)
        sides.append(upper_side)
    return jnp.stack(sides, axis=-1).astype(jnp.int32)


def block_scale(key, dims, shards, low, high):
    level, own = 1.0, jax.random.fold_in(key, 6)
    for axis_at, parts in shards:
        heights = jnp.exp(jax.random.uniform(jax.random.fold_in(own, axis_at), (parts,), jnp.float32, low / len(shards), high / len(shards)))
        level = level * jnp.repeat(heights, dims[axis_at] // parts).reshape([-1 if axis == axis_at else 1 for axis in range(len(dims))])
    return level


def centred(rng, extent, scale, bound, cuts=(), held_as=jnp.bfloat16):
    result = scale * jax.random.normal(rng, extent, jnp.float32)
    if cuts:
        result = result * block_scale(rng, extent, cuts, -0.22, 0.18)
    return jnp.clip(result, -bound, bound).astype(held_as)


def setup_inputs(seed: int = 0) -> dict:
    key_list = jax.random.split(jax.random.key(seed), 6)
    return {
        "rhs": draw_rhs(jax.random.fold_in(key_list[5], 71), 0),
        "vol_jac": centred(key_list[1], (NX, NY, NZ, BLK, BLK), BLK ** -0.5, 0.3125, ((0, 32), (1, 8)), jnp.float32),
        "inv_step": jnp.clip(jnp.exp(math.log(16.0) - 1.3862944 * jax.random.uniform(key_list[2], (NX, NY, NZ), jnp.float32) ** block_scale(key_list[2], (NX, NY, NZ), ((0, 32), (1, 8)), -0.2, 0.2)), 4.0, 16.0),
        "face_jac": jnp.clip(jax.random.uniform(key_list[3], (NX, NY, NZ, 6, NV, NV), jnp.float32, -1.0, 1.0) * block_scale(key_list[3], (NX, NY, NZ, 6, NV, NV), ((0, 32), (1, 8)), -0.4, 0.0), -1.0, 1.0),
        "orientation": draw_orientation(jax.random.fold_in(key_list[5], 71), 0),
    }


penalty = 4.0
highest = lax.Precision.HIGHEST

def face_tables(nodes_side):
    node_count = nodes_side ** 3
    across = nodes_side * nodes_side
    selector = np.zeros((6, node_count, across), np.float32)
    for face_id in range(6):
        for node_id in range(node_count):
            first_coord = node_id % nodes_side
            second_coord = node_id // nodes_side % nodes_side
            third_coord = node_id // across
            fixed_axis = [first_coord, first_coord, second_coord, second_coord, third_coord, third_coord][face_id]
            target = 0 if face_id % 2 == 0 else nodes_side - 1
            if fixed_axis == target:
                plane_pair = [(second_coord, third_coord), (second_coord, third_coord), (first_coord, third_coord), (first_coord, third_coord), (first_coord, second_coord), (first_coord, second_coord)][face_id]
                selector[face_id, node_id, plane_pair[0] + nodes_side * plane_pair[1]] = 1.0
    turning = np.zeros((8, across, across), np.float32)
    for orient_code in range(8):
        for face_node in range(across):
            along_first = face_node % nodes_side
            along_second = face_node // nodes_side
            if orient_code & 4:
                along_first, along_second = (along_second, along_first)
            if orient_code & 1:
                along_first = nodes_side - 1 - along_first
            if orient_code & 2:
                along_second = nodes_side - 1 - along_second
            turning[orient_code, face_node, along_first + nodes_side * along_second] = 1.0
    return (selector, turning)

def element_traces(operand, selector):
    shaped = operand.reshape(operand.shape[:-1] + (NV, NP))
    return jnp.einsum('...vn,fnq->...fvq', shaped, selector, precision=highest)

def lift_faces(face_values, selector):
    lifted = jnp.einsum('...fvq,fnq->...vn', face_values, selector, precision=highest)
    return lifted.reshape(lifted.shape[:-2] + (NV * NP,))

def face_terms(own_traces, oriented, face_jac):
    identity = jnp.eye(NV, dtype=jnp.float32)
    own_part = jnp.einsum('...fij,...fjq->...fiq', face_jac + penalty * identity, own_traces, precision=highest)
    other_part = jnp.einsum('...fij,...fjq->...fiq', face_jac - penalty * identity, oriented, precision=highest)
    return 0.5 * (own_part + other_part)

def invert_blocks(vol_jac, inv_step, face_jac, selector):
    eye_nodes = jnp.eye(NP, dtype=jnp.float32)
    eye_block = jnp.eye(NV * NP, dtype=jnp.float32)
    coverage = lax.optimization_barrier(jnp.sum(selector, axis=-1))
    own_face = 0.5 * (face_jac + penalty * jnp.eye(NV, dtype=jnp.float32))
    node_part = jnp.einsum('...fij,fn->...ijn', own_face, coverage, precision=highest)
    face_block = jnp.einsum('...ijn,nm->...injm', node_part, eye_nodes, precision=highest)
    face_block = face_block.reshape(face_block.shape[:-4] + (NV * NP, NV * NP))
    element_block = vol_jac + face_block + inv_step[..., None, None] * eye_block
    diagonal = jnp.diagonal(element_block, axis1=-2, axis2=-1)
    approx = eye_block * (1.0 / diagonal)[..., :, None]
    for sweep_id in range(NS_STEPS):
        product = jnp.einsum('...rk,...kc->...rc', element_block, approx, precision=highest)
        approx = 2.0 * approx - jnp.einsum('...rk,...kc->...rc', approx, product, precision=highest)
    return approx

def apply_precond(precond, operand):
    return jnp.einsum('...rc,...c->...r', precond, operand, precision=highest)

def apply_jacobian(operand, vol_jac, inv_step, face_jac, orient_mats, selector):
    own_traces = element_traces(operand, selector)
    roll_moves = [(1, 0), (-1, 0), (1, 1), (-1, 1), (1, 2), (-1, 2)]
    gathered = []
    for face_id in range(6):
        shifted = jnp.roll(own_traces, roll_moves[face_id][0], axis=roll_moves[face_id][1])
        gathered.append(shifted[:, :, :, face_id ^ 1])
    neighbours = jnp.stack(gathered, axis=3)
    oriented = jnp.einsum('...fqp,...fvp->...fvq', orient_mats, neighbours, precision=highest)
    coupled = face_terms(own_traces, oriented, face_jac)
    volume = jnp.einsum('...rc,...c->...r', vol_jac, operand, precision=highest)
    return inv_step[..., None] * operand + volume + lift_faces(coupled, selector)

def least_squares(columns, initial_norm):
    steps_count = len(columns)
    rotations = []
    target_values = [initial_norm] + [jnp.zeros_like(initial_norm)] * steps_count
    upper_rows = []
    for column_id in range(steps_count):
        column = list(columns[column_id])
        for index_id in range(column_id):
            cosine, sine_part = rotations[index_id]
            top_value = cosine * column[index_id] + sine_part * column[index_id + 1]
            column[index_id + 1] = -sine_part * column[index_id] + cosine * column[index_id + 1]
            column[index_id] = top_value
        radius = jnp.sqrt(column[column_id] * column[column_id] + column[column_id + 1] * column[column_id + 1])
        cosine = column[column_id] / radius
        sine_part = column[column_id + 1] / radius
        rotations.append((cosine, sine_part))
        column[column_id] = radius
        target_values[column_id + 1] = -sine_part * target_values[column_id]
        target_values[column_id] = cosine * target_values[column_id]
        upper_rows.append(column)
    coefficients = [None] * steps_count
    for row_id in reversed(range(steps_count)):
        running = target_values[row_id]
        for later_id in range(row_id + 1, steps_count):
            running = running - upper_rows[later_id][row_id] * coefficients[later_id]
        coefficients[row_id] = running / upper_rows[row_id][row_id]
    return (coefficients, jnp.abs(target_values[steps_count]) / initial_norm)

def reference(rhs, vol_jac, inv_step, face_jac, orientation):
    selector_np, turning_np = face_tables(Q)
    selector = jnp.asarray(selector_np)
    turning = jnp.asarray(turning_np)

    def invert_slab(slab_args):
        return invert_blocks(slab_args[0], slab_args[1], slab_args[2], selector)
    precond = lax.map(invert_slab, (vol_jac, inv_step, face_jac))
    orient_hot = (orientation[..., None] == jnp.arange(8, dtype=jnp.int32)).astype(jnp.float32)
    orient_mats = jnp.einsum('...fo,oqp->...fqp', orient_hot, turning, precision=highest)
    initial_norm = jnp.sqrt(jnp.sum(rhs * rhs))
    krylov_basis = [rhs / initial_norm]
    directions = []
    columns = []
    for iteration in range(ITERS):
        direction = apply_precond(precond, krylov_basis[-1])
        directions.append(direction)
        image_vec = apply_jacobian(direction, vol_jac, inv_step, face_jac, orient_mats, selector)
        column = []
        for vector in krylov_basis:
            projection = jnp.sum(image_vec * vector)
            image_vec = image_vec - projection * vector
            column.append(projection)
        new_norm = jnp.sqrt(jnp.sum(image_vec * image_vec))
        column.append(new_norm)
        columns.append(column)
        krylov_basis.append(image_vec / new_norm)
    coefficients, residual_ratio = least_squares(columns, initial_norm)
    update = coefficients[0] * directions[0]
    for index_id in range(1, ITERS):
        update = update + coefficients[index_id] * directions[index_id]
    return (update, residual_ratio)
```

```python
import jax
import jax.numpy as jnp
import numpy as np
from jax import lax
from jax.experimental import pallas as pl
from jax.experimental.pallas import tpu as pltpu
from jax.sharding import PartitionSpec as P

Q = 4
NV = 5
ITERS = 3
NS_STEPS = 3
NP = 64


penalty = 4.0
highest = lax.Precision.HIGHEST


def extended(shard, sides, width):
    for axis, dim in sides:
        size, length = (lax.axis_size(axis), shard.shape[dim])
        up = [(i, (i + 1) % size) for i in range(size)]
        down = [(j, i) for i, j in up]
        last = lax.slice_in_dim(shard, length - width, length, axis=dim)
        first = lax.slice_in_dim(shard, 0, width, axis=dim)
        before = lax.ppermute(last, axis, up)
        after = lax.ppermute(first, axis, down)
        shard = jnp.concatenate([before, shard, after], axis=dim)
    return shard


def face_tables(nodes_side):
    node_count = nodes_side**3
    across = nodes_side * nodes_side
    selector = np.zeros((6, node_count, across), np.float32)
    for face_id in range(6):
        for node_id in range(node_count):
            first_coord = node_id % nodes_side
            second_coord = node_id // nodes_side % nodes_side
            third_coord = node_id // across
            fixed_axis = [
                first_coord,
                first_coord,
                second_coord,
                second_coord,
                third_coord,
                third_coord,
            ][face_id]
            target = 0 if face_id % 2 == 0 else nodes_side - 1
            if fixed_axis == target:
                plane_pair = [
                    (second_coord, third_coord),
                    (second_coord, third_coord),
                    (first_coord, third_coord),
                    (first_coord, third_coord),
                    (first_coord, second_coord),
                    (first_coord, second_coord),
                ][face_id]
                selector[face_id, node_id, plane_pair[0] + nodes_side * plane_pair[1]] = 1.0
    turning = np.zeros((8, across, across), np.float32)
    for orient_code in range(8):
        for face_node in range(across):
            along_first = face_node % nodes_side
            along_second = face_node // nodes_side
            if orient_code & 4:
                along_first, along_second = (along_second, along_first)
            if orient_code & 1:
                along_first = nodes_side - 1 - along_first
            if orient_code & 2:
                along_second = nodes_side - 1 - along_second
            turning[orient_code, face_node, along_first + nodes_side * along_second] = 1.0
    return (selector, turning)


def element_traces(operand, selector):
    shaped = operand.reshape(operand.shape[:-1] + (NV, NP))
    return jnp.einsum("...vn,fnq->...fvq", shaped, selector, precision=highest)


def lift_faces(face_values, selector):
    lifted = jnp.einsum("...fvq,fnq->...vn", face_values, selector, precision=highest)
    return lifted.reshape(lifted.shape[:-2] + (NV * NP,))


def face_terms(own_traces, oriented, face_jac):
    identity = jnp.eye(NV, dtype=jnp.float32)
    own_part = jnp.einsum(
        "...fij,...fjq->...fiq", face_jac + penalty * identity, own_traces, precision=highest
    )
    other_part = jnp.einsum(
        "...fij,...fjq->...fiq", face_jac - penalty * identity, oriented, precision=highest
    )
    return 0.5 * (own_part + other_part)


def invert_blocks(vol_jac, inv_step, face_jac, selector):
    eye_nodes = jnp.eye(NP, dtype=jnp.float32)
    eye_block = jnp.eye(NV * NP, dtype=jnp.float32)
    coverage = jnp.sum(selector, axis=-1)
    own_face = 0.5 * (face_jac + penalty * jnp.eye(NV, dtype=jnp.float32))
    node_part = jnp.einsum("...fij,fn->...ijn", own_face, coverage, precision=highest)
    face_block = jnp.einsum("...ijn,nm->...injm", node_part, eye_nodes, precision=highest)
    face_block = face_block.reshape(face_block.shape[:-4] + (NV * NP, NV * NP))
    element_block = vol_jac + face_block + inv_step[..., None, None] * eye_block
    diagonal = jnp.diagonal(element_block, axis1=-2, axis2=-1)
    approx = eye_block * (1.0 / diagonal)[..., :, None]
    for sweep_id in range(NS_STEPS):
        product = jnp.einsum("...rk,...kc->...rc", element_block, approx, precision=highest)
        approx = 2.0 * approx - jnp.einsum("...rk,...kc->...rc", approx, product, precision=highest)
    return approx


def apply_precond(precond, operand):
    return jnp.einsum("...rc,...c->...r", precond, operand, precision=highest)


def apply_jacobian(operand, vol_jac, inv_step, face_jac, orient_mats, selector):
    own_traces = element_traces(operand, selector)
    padded = extended(operand, (("gx", 0), ("gy", 1)), 1)
    padded_traces = element_traces(padded, selector)
    side_faces = [
        padded_traces[0:-2, 1:-1, :, 1],
        padded_traces[2:, 1:-1, :, 0],
        padded_traces[1:-1, 0:-2, :, 3],
        padded_traces[1:-1, 2:, :, 2],
    ]
    lower_face = jnp.roll(own_traces, 1, axis=2)[:, :, :, 5]
    upper_face = jnp.roll(own_traces, -1, axis=2)[:, :, :, 4]
    neighbours = jnp.stack(side_faces + [lower_face, upper_face], axis=3)
    oriented = jnp.einsum("...fqp,...fvp->...fvq", orient_mats, neighbours, precision=highest)
    coupled = face_terms(own_traces, oriented, face_jac)
    volume = jnp.einsum("...rc,...c->...r", vol_jac, operand, precision=highest)
    return inv_step[..., None] * operand + volume + lift_faces(coupled, selector)


def least_squares(columns, initial_norm):
    steps_count = len(columns)
    rotations = []
    target_values = [initial_norm] + [jnp.zeros_like(initial_norm)] * steps_count
    upper_rows = []
    for column_id in range(steps_count):
        column = list(columns[column_id])
        for index_id in range(column_id):
            cosine, sine_part = rotations[index_id]
            top_value = cosine * column[index_id] + sine_part * column[index_id + 1]
            column[index_id + 1] = -sine_part * column[index_id] + cosine * column[index_id + 1]
            column[index_id] = top_value
        radius = jnp.sqrt(
            column[column_id] * column[column_id] + column[column_id + 1] * column[column_id + 1]
        )
        cosine = column[column_id] / radius
        sine_part = column[column_id + 1] / radius
        rotations.append((cosine, sine_part))
        column[column_id] = radius
        target_values[column_id + 1] = -sine_part * target_values[column_id]
        target_values[column_id] = cosine * target_values[column_id]
        upper_rows.append(column)
    coefficients = [None] * steps_count
    for row_id in reversed(range(steps_count)):
        running = target_values[row_id]
        for later_id in range(row_id + 1, steps_count):
            running = running - upper_rows[later_id][row_id] * coefficients[later_id]
        coefficients[row_id] = running / upper_rows[row_id][row_id]
    return (coefficients, jnp.abs(target_values[steps_count]) / initial_norm)


def careful(rhs, vol_jac, inv_step, face_jac, orientation):
    selector_np, turning_np = face_tables(Q)
    selector = jnp.asarray(selector_np)
    turning = jnp.asarray(turning_np)
    initial_norm = jnp.sqrt(lax.psum(jnp.sum(rhs * rhs), ("gx", "gy")))
    precond = invert_blocks(vol_jac, inv_step, face_jac, selector)
    orient_hot = (orientation[..., None] == jnp.arange(8, dtype=jnp.int32)).astype(jnp.float32)
    orient_mats = jnp.einsum("...fo,oqp->...fqp", orient_hot, turning, precision=highest)
    krylov_basis = [rhs / initial_norm]
    directions = []
    columns = []
    for iteration in range(ITERS):
        direction = apply_precond(precond, krylov_basis[-1])
        directions.append(direction)
        image_vec = apply_jacobian(direction, vol_jac, inv_step, face_jac, orient_mats, selector)
        column = []
        for vector in krylov_basis:
            projection = lax.psum(jnp.sum(image_vec * vector), ("gx", "gy"))
            image_vec = image_vec - projection * vector
            column.append(projection)
        new_norm = jnp.sqrt(lax.psum(jnp.sum(image_vec * image_vec), ("gx", "gy")))
        column.append(new_norm)
        columns.append(column)
        krylov_basis.append(image_vec / new_norm)
    coefficients, residual_ratio = least_squares(columns, initial_norm)
    update = coefficients[0] * directions[0]
    for index_id in range(1, ITERS):
        update = update + coefficients[index_id] * directions[index_id]
    return (update, residual_ratio)


EL = 4
BLK = NV * NP
LANES = 128
TILES = 3
WIDE = TILES * LANES
GROUPS = BLK // 8
MIN_PIVOT = 0.02
MIN_SCALE = 1e-18
MAX_SCALE = 1e30
DEVICES_AXES = ("gx", "gy")


def tile_iota(dim):
    return lax.broadcasted_iota(jnp.int32, (8, LANES), dim)


def turn(x, shift):
    return pltpu.roll(x, shift % 8, 0)


def pick(x, index):
    return jnp.take_along_axis(x, index, axis=1)


def split(x):
    return [x[:, t * LANES : (t + 1) * LANES] for t in range(TILES)]


def face_of_row(pair):
    return 2 * pair + (tile_iota(0) >> 2)


def collect(per_element):
    row = tile_iota(0)
    even = (row & 1) == 0
    low = (row & 2) == 0
    folded = [a + turn(a, 4) for a in per_element]

    def join(mask, first, second, step):
        return jnp.where(mask, first, second) + turn(jnp.where(mask, second, first), -step)

    return join(low, join(even, folded[0], folded[1], 1), join(even, folded[2], folded[3], 1), 2)


def row_masks():
    offset = tile_iota(1) - tile_iota(0)
    return [offset == 8 * k for k in range(LANES // 8)]


def couple_rows(f_ref, y):
    masks = row_masks()
    tiles = [[] for _ in range(TILES)]
    for e in range(EL):
        spread = [jnp.broadcast_to(part[e : e + 1, :], (8, LANES)) for part in y]
        acc = [jnp.zeros((8, LANES), jnp.float32) for _ in range(TILES)]
        for g in range(GROUPS):
            rows = slice(8 * g, 8 * g + 8)
            p = f_ref[e, rows, 0:LANES] * spread[0]
            p = p + f_ref[e, rows, LANES : 2 * LANES] * spread[1]
            p = p + f_ref[e, rows, 2 * LANES : WIDE] * spread[2]
            total = jnp.sum(p, axis=1, keepdims=True)
            t, k = divmod(g, LANES // 8)
            acc[t] = jnp.where(masks[k], total, acc[t])
        for t in range(TILES):
            tiles[t].append(acc[t])
    return [collect(parts) for parts in tiles]


def series(f_ref, start, inverse):
    def step(_, y):
        moved = couple_rows(f_ref, y)
        return tuple(inverse[t] * (start[t] + moved[t]) for t in range(TILES))

    first = tuple(inverse[t] * start[t] for t in range(TILES))
    return list(lax.fori_loop(0, 2**NS_STEPS - 1, step, first))


def traces_of(z):
    lane = tile_iota(1)
    var, node = lane >> 4, lane & 15
    s, t = node & 3, node >> 2
    result = []
    for pair in range(3):
        if pair == 0:
            place = 4 * s + 16 * t + 3 * (tile_iota(0) >> 2)
        elif pair == 1:
            place = s + 16 * t + 12 * (tile_iota(0) >> 2)
        else:
            place = s + 4 * t + 48 * (tile_iota(0) >> 2)
        index = (var & 1) * NP + place
        parts = [pick(z[k], index) for k in range(TILES)]
        tile = var >> 1
        result.append(jnp.where(tile == 0, parts[0], jnp.where(tile == 1, parts[1], parts[2])))
    return result


def turned_nodes(code):
    node = tile_iota(1) & 15
    s, t = node & 3, node >> 2
    swap = (code & 4) != 0
    first = jnp.where(swap, t, s)
    second = jnp.where(swap, s, t)
    first = jnp.where((code & 1) != 0, 3 - first, first)
    second = jnp.where((code & 2) != 0, 3 - second, second)
    return first + 4 * second


def through_faces(pair, neighbour, g_ref, q_ref):
    lane = tile_iota(1)
    own = lane >> 4
    turned = q_ref[pair]
    value = None
    for shift in range(NV):
        other = own + shift
        other = jnp.where(other >= NV, other - NV, other)
        index = (other * 16 + turned) & (LANES - 1)
        term = g_ref[3 * shift + pair] * pick(neighbour, index)
        value = term if value is None else value + term
    node = lane & (NP - 1)
    a, b, c = node & 3, (node >> 2) & 3, node >> 4
    end = 3 * (tile_iota(0) >> 2)
    if pair == 0:
        hit, place = a == end, b + 4 * c
    elif pair == 1:
        hit, place = b == end, a + 4 * c
    else:
        hit, place = c == end, a + 4 * b
    lifted = []
    for t in range(TILES):
        index = ((2 * t + (lane >> 6)) * 16 + place) & (LANES - 1)
        keep = hit if t < 2 else hit & (lane < NP)
        lifted.append(jnp.where(keep, pick(value, index), 0.0))
    return lifted


def fold(parts):
    return [p + turn(p, 4) for p in parts]


def across_third(trace):
    row = tile_iota(0)
    inner = jnp.where(row < 4, turn(trace, -3), turn(trace, 3))
    outer = jnp.where(row == 0, turn(trace, 1), turn(trace, -1))
    return jnp.where((row == 0) | (row == 7), outer, inner)


def put(ref, parts):
    for t in range(TILES):
        ref[:, t * LANES : (t + 1) * LANES] = parts[t]


def prepare(vol_ref, rhs_ref, inv_ref, fj_ref, ori_ref, f_ref, d_ref, g_ref, q_ref, r_ref, z_ref, tx_ref, ty_ref, tz_ref):
    row, lane = tile_iota(0), tile_iota(1)
    zero = jnp.zeros((8, LANES), jnp.float32)
    r_ref[...] = jnp.zeros((8, WIDE), jnp.float32)
    r_ref[0:4, 0:BLK] = rhs_ref[...]
    r_ref[4:8, 0:BLK] = rhs_ref[...]
    start = split(r_ref[...])
    d_ref[...] = jnp.zeros((8, WIDE), jnp.float32)
    d_ref[0:4, 0:6] = ori_ref[...].astype(jnp.float32)
    d_ref[4:8, 0:6] = ori_ref[...].astype(jnp.float32)
    codes = d_ref[:, 0:LANES]
    for pair in range(3):
        q_ref[pair] = turned_nodes(pick(codes, face_of_row(pair)).astype(jnp.int32))
    packed = []
    for i in range(NV):
        total = zero
        for j in range(NV):
            d_ref[:, 0:LANES] = zero
            d_ref[0:4, 0:6] = fj_ref[i, j]
            d_ref[4:8, 0:6] = fj_ref[i, j]
            part = d_ref[:, 0:LANES]
            total = total + (part if j == 0 else pltpu.roll(part, 16 * j, 1))
        packed.append(total)
    own = lane >> 4
    for shift in range(NV):
        other = own + shift
        other = jnp.where(other >= NV, other - NV, other)
        for pair in range(3):
            index = (other * 16 + face_of_row(pair)) & (LANES - 1)
            value = zero
            for i in range(NV):
                value = jnp.where(own == i, pick(packed[i], index), value)
            if shift == 0:
                value = value - penalty
            g_ref[3 * shift + pair] = jnp.where(own < NV, 0.5 * value, 0.0)
    node = lane & (NP - 1)
    a, b, c = node & 3, (node >> 2) & 3, node >> 4
    cover = [a == 0, a == 3, b == 0, b == 3, c == 0, c == 3]
    node_part = []
    for i in range(NV):
        tiles = []
        for t in range(TILES):
            var = 2 * t + (lane >> 6)
            index = (var * 16) & (LANES - 1)
            value = zero
            for f in range(6):
                term = pick(packed[i], index + f)
                term = term + jnp.where(var == i, penalty, 0.0)
                value = value + jnp.where(cover[f], 0.5 * term, 0.0)
            if t == 2:
                value = jnp.where(lane < NP, value, 0.0)
            tiles.append(value)
        node_part.append(tiles)
    shifts = zero
    for e in range(EL):
        shifts = jnp.where((row & 3) == e, inv_ref[e], shifts)
    masks = row_masks()
    node_offset = node - row
    diag_tiles = [[] for _ in range(TILES)]
    for e in range(EL):
        acc = [zero for _ in range(TILES)]
        for i in range(NV):
            spread = [jnp.broadcast_to(node_part[i][t][e : e + 1, :], (8, LANES)) for t in range(TILES)]
            for gi in range(NP // 8):
                g = i * (NP // 8) + gi
                rows = slice(8 * g, 8 * g + 8)
                td, k = divmod(g, LANES // 8)
                same_node = node_offset == 8 * gi
                for t in range(TILES):
                    if t < 2:
                        vol = vol_ref[e, rows, t * LANES : (t + 1) * LANES]
                        value = -vol - jnp.where(same_node, spread[t], 0.0)
                        if t == td:
                            acc[t] = jnp.where(masks[k], value, acc[t])
                            value = jnp.where(masks[k], 0.0, value)
                        f_ref[e, rows, t * LANES : (t + 1) * LANES] = value
                    else:
                        value = jnp.concatenate([vol_ref[e, rows, 2 * LANES : BLK], jnp.zeros((8, WIDE - BLK), jnp.float32)], axis=1)
                        value = -value - jnp.where(same_node, spread[t], 0.0)
                        if t == td:
                            acc[t] = jnp.where(masks[k], value, acc[t])
                            value = jnp.where(masks[k], 0.0, value)
                        f_ref[e, rows, 2 * LANES : WIDE] = value
        for t in range(TILES):
            diag_tiles[t].append(acc[t])
    diag = [shifts - collect(parts) for parts in diag_tiles]
    diag[2] = jnp.where(lane < NP, diag[2], 1.0)
    put(d_ref, diag)
    z = series(f_ref, start, [1.0 / x for x in diag])
    put(z_ref, z)
    tx_ref[...], ty_ref[...], tz_ref[...] = traces_of(z)


def own_part(f_ref, d_ref, g_ref, q_ref, r_ref, z_ref, tz_ref, out_ref):
    r, z, diag = split(r_ref[...]), split(z_ref[...]), split(d_ref[...])
    moved = couple_rows(f_ref, z)
    third = fold(through_faces(2, across_third(tz_ref[...]), g_ref, q_ref))
    put(out_ref, [diag[t] * z[t] - moved[t] - r[t] + third[t] for t in range(TILES)])


def arrived(side_ref, own_axis, pair_ref, far_ref):
    odd = side_ref[own_axis] == 1
    near, far = pair_ref[...], far_ref[...]
    before = jnp.where(odd, near, far)
    after = jnp.where(odd, far, near)
    return turn(jnp.where(tile_iota(0) >= 4, before, after), 4)


def next_vector(side_ref, part_ref, c_ref, z_ref, x_ref, y_ref, g_ref, q_ref):
    first = through_faces(0, arrived(side_ref, 0, c_ref, z_ref), g_ref, q_ref)
    second = through_faces(1, arrived(side_ref, 1, x_ref, y_ref), g_ref, q_ref)
    lifted = fold([first[t] + second[t] for t in range(TILES)])
    part = split(part_ref[...])
    return [part[t] + lifted[t] for t in range(TILES)]


def advance(side_ref, part_ref, rc_ref, rz_ref, rx_ref, ry_ref, g_ref, q_ref, f_ref, d_ref, r_ref, z_ref, tx_ref, ty_ref, tz_ref):
    r = next_vector(side_ref, part_ref, rc_ref, rz_ref, rx_ref, ry_ref, g_ref, q_ref)
    put(r_ref, r)
    z = series(f_ref, r, [1.0 / x for x in split(d_ref[...])])
    put(z_ref, z)
    tx_ref[...], ty_ref[...], tz_ref[...] = traces_of(z)


def products(side_ref, part_ref, rc_ref, rz_ref, rx_ref, ry_ref, g_ref, q_ref, r0_ref, r1_ref, r2_ref, out_ref):
    last = next_vector(side_ref, part_ref, rc_ref, rz_ref, rx_ref, ry_ref, g_ref, q_ref)
    basis = [split(r0_ref[...]), split(r1_ref[...]), split(r2_ref[...]), last]
    lane = tile_iota(1)
    acc = jnp.zeros((8, LANES), jnp.float32)
    slot = 0
    for i in range(ITERS + 1):
        for j in range(i + 1):
            p = basis[i][0] * basis[j][0] + basis[i][1] * basis[j][1] + basis[i][2] * basis[j][2]
            acc = jnp.where(lane == slot, jnp.sum(p, axis=1, keepdims=True), acc)
            slot += 1
    for step in (1, 2):
        acc = acc + turn(acc, step)
    for n in range(out_ref.shape[0] // 8):
        out_ref[8 * n : 8 * n + 8, :] = acc


def finish(sums_ref, z1_ref, z2_ref, z3_ref, out_ref, ratio_ref):
    acc = jnp.zeros((8, LANES), jnp.float32)
    parts = [acc] * 4
    for n in range(sums_ref.shape[0] // 8):
        parts[n % 4] = parts[n % 4] + sums_ref[8 * n : 8 * n + 8, :]
    acc = (parts[0] + parts[1]) + (parts[2] + parts[3])
    for step in (1, 2, 4):
        acc = acc + turn(acc, step)
    gram = {}
    slot = 0
    for i in range(ITERS + 1):
        for j in range(i + 1):
            gram[j, i] = pick(acc, jnp.full((8, LANES), slot, jnp.int32))
            slot += 1
    upper = {}
    good = (gram[0, 0] > MIN_SCALE) & (gram[0, 0] < MAX_SCALE)
    for i in range(ITERS + 1):
        pivot = gram[i, i]
        for k in range(i):
            pivot = pivot - upper[k, i] * upper[k, i]
        good = good & (pivot > MIN_PIVOT * gram[i, i]) & (gram[i, i] > MIN_SCALE) & (gram[i, i] < MAX_SCALE)
        upper[i, i] = jnp.sqrt(pivot)
        inverse = 1.0 / upper[i, i]
        for j in range(i + 1, ITERS + 1):
            value = gram[i, j]
            for k in range(i):
                value = value - upper[k, i] * upper[k, j]
            upper[i, j] = value * inverse
    columns = []
    for j in range(1, ITERS + 1):
        column = [upper[i, j] + upper[i, j - 1] for i in range(j)]
        columns.append(column + [upper[j, j]])
    coefficients, ratio = least_squares(columns, upper[0, 0])
    z = [split(z1_ref[...]), split(z2_ref[...]), split(z3_ref[...])]
    for t in range(TILES):
        value = coefficients[0] * z[0][t] + coefficients[1] * z[1][t] + coefficients[2] * z[2][t]
        if t < 2:
            out_ref[:, t * LANES : (t + 1) * LANES] = value[0:EL, :]
        else:
            out_ref[:, 2 * LANES : BLK] = value[0:EL, 0 : BLK - 2 * LANES]
    lane = tile_iota(1)
    ratio_ref[...] = jnp.where(lane == 0, ratio, jnp.where(good, 1.0, 0.0))


def shape(*dims, dtype=jnp.float32):
    return jax.ShapeDtypeStruct(dims, dtype)


def call(kernel, outs, args, scalar_args=()):
    in_specs = [
        pl.BlockSpec(memory_space=pltpu.SMEM if n in scalar_args else pltpu.VMEM)
        for n in range(len(args))
    ]
    out_specs = jax.tree.map(lambda _: pl.BlockSpec(memory_space=pltpu.VMEM), outs)
    return pl.pallas_call(
        kernel,
        out_shape=outs,
        in_specs=in_specs,
        out_specs=out_specs,
        compiler_params=pltpu.CompilerParams(vmem_limit_bytes=24 * 2**20),
    )(*args)


def body(rhs, vol_jac, inv_step, face_jac, orientation):
    nx, ny = lax.axis_size("gx"), lax.axis_size("gy")
    flat = [(x, y) for x in range(nx) for y in range(ny)]

    def pairs(move):
        return [(x * ny + y, (move(x, y)[0] % nx) * ny + move(x, y)[1] % ny) for x, y in flat]

    routes = [
        pairs(lambda x, y: (x ^ 1, y)),
        pairs(lambda x, y: (x, y ^ 1)),
        pairs(lambda x, y: (x, y + 1 if y % 2 else y - 1)),
        pairs(lambda x, y: (x + 1 if x % 2 else x - 1, y)),
    ]

    def exchange(tx, ty):
        near_x = lax.ppermute(tx, DEVICES_AXES, routes[0])
        near_y = lax.ppermute(ty, DEVICES_AXES, routes[1])
        far_y = lax.ppermute(ty, DEVICES_AXES, routes[2])
        far_x = lax.ppermute(tx, DEVICES_AXES, routes[3])
        return near_x, far_x, near_y, far_y

    side = jnp.stack([lax.axis_index("gx") % 2, lax.axis_index("gy") % 2]).astype(jnp.int32)
    vec, tr = shape(8, WIDE), shape(8, LANES)
    matrix, diag, g, q, r0, z, tx, ty, tz = call(
        prepare,
        (shape(EL, BLK, WIDE), vec, shape(3 * NV, 8, LANES), shape(3, 8, LANES, dtype=jnp.int32), vec, vec, tr, tr, tr),
        (
            vol_jac.reshape(EL, BLK, BLK),
            rhs.reshape(EL, BLK),
            inv_step.reshape(EL),
            face_jac.reshape(EL, 6, NV, NV).transpose(2, 3, 0, 1),
            orientation.reshape(EL, 6),
        ),
        scalar_args=(2,),
    )
    basis, directions = [r0], [z]
    for iteration in range(ITERS):
        around = exchange(tx, ty)
        part = call(own_part, vec, (matrix, diag, g, q, basis[-1], z, tz))
        if iteration < ITERS - 1:
            r, z, tx, ty, tz = call(
                advance, (vec, vec, tr, tr, tr), (side, part, *around, g, q, matrix, diag), scalar_args=(0,)
            )
            basis.append(r)
            directions.append(z)
    total = nx * ny
    sums = call(products, shape(total, LANES), (side, part, *around, g, q, *basis), scalar_args=(0,))
    sums = lax.all_to_all(sums.reshape(total, 1, LANES), DEVICES_AXES, 0, 0).reshape(total, LANES)
    update, ratio = call(finish, (shape(EL, BLK), tr), (sums, *directions))
    fine = ratio[0, 1] > 0.5
    return lax.cond(
        fine,
        lambda: (update.reshape(rhs.shape), ratio[0, 0]),
        lambda: careful(rhs, vol_jac, inv_step, face_jac, orientation),
    )


def solution(mesh):
    placed = (
        P("gx", "gy", None, None),
        P("gx", "gy", None, None, None),
        P("gx", "gy", None),
        P("gx", "gy", None, None, None, None),
        P("gx", "gy", None, None),
    )
    return jax.shard_map(
        body,
        mesh=mesh,
        in_specs=placed,
        out_specs=(P("gx", "gy", None, None), P()),
        check_vma=False,
    )
```

```python
import jax
import jax.numpy as jnp
import numpy as np
from jax import lax
from jax.experimental import pallas as pl
from jax.experimental.pallas import tpu as pltpu
from jax.sharding import PartitionSpec as P

Q = 4
NV = 5
ITERS = 3
NS_STEPS = 3
NP = 64


penalty = 4.0
highest = lax.Precision.HIGHEST


def extended(shard, sides, width):
    for axis, dim in sides:
        size, length = (lax.axis_size(axis), shard.shape[dim])
        up = [(i, (i + 1) % size) for i in range(size)]
        down = [(j, i) for i, j in up]
        last = lax.slice_in_dim(shard, length - width, length, axis=dim)
        first = lax.slice_in_dim(shard, 0, width, axis=dim)
        before = lax.ppermute(last, axis, up)
        after = lax.ppermute(first, axis, down)
        shard = jnp.concatenate([before, shard, after], axis=dim)
    return shard


def face_tables(nodes_side):
    node_count = nodes_side**3
    across = nodes_side * nodes_side
    selector = np.zeros((6, node_count, across), np.float32)
    for face_id in range(6):
        for node_id in range(node_count):
            first_coord = node_id % nodes_side
            second_coord = node_id // nodes_side % nodes_side
            third_coord = node_id // across
            fixed_axis = [
                first_coord,
                first_coord,
                second_coord,
                second_coord,
                third_coord,
                third_coord,
            ][face_id]
            target = 0 if face_id % 2 == 0 else nodes_side - 1
            if fixed_axis == target:
                plane_pair = [
                    (second_coord, third_coord),
                    (second_coord, third_coord),
                    (first_coord, third_coord),
                    (first_coord, third_coord),
                    (first_coord, second_coord),
                    (first_coord, second_coord),
                ][face_id]
                selector[face_id, node_id, plane_pair[0] + nodes_side * plane_pair[1]] = 1.0
    turning = np.zeros((8, across, across), np.float32)
    for orient_code in range(8):
        for face_node in range(across):
            along_first = face_node % nodes_side
            along_second = face_node // nodes_side
            if orient_code & 4:
                along_first, along_second = (along_second, along_first)
            if orient_code & 1:
                along_first = nodes_side - 1 - along_first
            if orient_code & 2:
                along_second = nodes_side - 1 - along_second
            turning[orient_code, face_node, along_first + nodes_side * along_second] = 1.0
    return (selector, turning)


def element_traces(operand, selector):
    shaped = operand.reshape(operand.shape[:-1] + (NV, NP))
    return jnp.einsum("...vn,fnq->...fvq", shaped, selector, precision=highest)


def lift_faces(face_values, selector):
    lifted = jnp.einsum("...fvq,fnq->...vn", face_values, selector, precision=highest)
    return lifted.reshape(lifted.shape[:-2] + (NV * NP,))


def face_terms(own_traces, oriented, face_jac):
    identity = jnp.eye(NV, dtype=jnp.float32)
    own_part = jnp.einsum(
        "...fij,...fjq->...fiq", face_jac + penalty * identity, own_traces, precision=highest
    )
    other_part = jnp.einsum(
        "...fij,...fjq->...fiq", face_jac - penalty * identity, oriented, precision=highest
    )
    return 0.5 * (own_part + other_part)


def invert_blocks(vol_jac, inv_step, face_jac, selector):
    eye_nodes = jnp.eye(NP, dtype=jnp.float32)
    eye_block = jnp.eye(NV * NP, dtype=jnp.float32)
    coverage = jnp.sum(selector, axis=-1)
    own_face = 0.5 * (face_jac + penalty * jnp.eye(NV, dtype=jnp.float32))
    node_part = jnp.einsum("...fij,fn->...ijn", own_face, coverage, precision=highest)
    face_block = jnp.einsum("...ijn,nm->...injm", node_part, eye_nodes, precision=highest)
    face_block = face_block.reshape(face_block.shape[:-4] + (NV * NP, NV * NP))
    element_block = vol_jac + face_block + inv_step[..., None, None] * eye_block
    diagonal = jnp.diagonal(element_block, axis1=-2, axis2=-1)
    approx = eye_block * (1.0 / diagonal)[..., :, None]
    for sweep_id in range(NS_STEPS):
        product = jnp.einsum("...rk,...kc->...rc", element_block, approx, precision=highest)
        approx = 2.0 * approx - jnp.einsum("...rk,...kc->...rc", approx, product, precision=highest)
    return approx


def apply_precond(precond, operand):
    return jnp.einsum("...rc,...c->...r", precond, operand, precision=highest)


def apply_jacobian(operand, vol_jac, inv_step, face_jac, orient_mats, selector):
    own_traces = element_traces(operand, selector)
    padded = extended(operand, (("gx", 0), ("gy", 1)), 1)
    padded_traces = element_traces(padded, selector)
    side_faces = [
        padded_traces[0:-2, 1:-1, :, 1],
        padded_traces[2:, 1:-1, :, 0],
        padded_traces[1:-1, 0:-2, :, 3],
        padded_traces[1:-1, 2:, :, 2],
    ]
    lower_face = jnp.roll(own_traces, 1, axis=2)[:, :, :, 5]
    upper_face = jnp.roll(own_traces, -1, axis=2)[:, :, :, 4]
    neighbours = jnp.stack(side_faces + [lower_face, upper_face], axis=3)
    oriented = jnp.einsum("...fqp,...fvp->...fvq", orient_mats, neighbours, precision=highest)
    coupled = face_terms(own_traces, oriented, face_jac)
    volume = jnp.einsum("...rc,...c->...r", vol_jac, operand, precision=highest)
    return inv_step[..., None] * operand + volume + lift_faces(coupled, selector)


def least_squares(columns, initial_norm):
    steps_count = len(columns)
    rotations = []
    target_values = [initial_norm] + [jnp.zeros_like(initial_norm)] * steps_count
    upper_rows = []
    for column_id in range(steps_count):
        column = list(columns[column_id])
        for index_id in range(column_id):
            cosine, sine_part = rotations[index_id]
            top_value = cosine * column[index_id] + sine_part * column[index_id + 1]
            column[index_id + 1] = -sine_part * column[index_id] + cosine * column[index_id + 1]
            column[index_id] = top_value
        radius = jnp.sqrt(
            column[column_id] * column[column_id] + column[column_id + 1] * column[column_id + 1]
        )
        cosine = column[column_id] / radius
        sine_part = column[column_id + 1] / radius
        rotations.append((cosine, sine_part))
        column[column_id] = radius
        target_values[column_id + 1] = -sine_part * target_values[column_id]
        target_values[column_id] = cosine * target_values[column_id]
        upper_rows.append(column)
    coefficients = [None] * steps_count
    for row_id in reversed(range(steps_count)):
        running = target_values[row_id]
        for later_id in range(row_id + 1, steps_count):
            running = running - upper_rows[later_id][row_id] * coefficients[later_id]
        coefficients[row_id] = running / upper_rows[row_id][row_id]
    return (coefficients, jnp.abs(target_values[steps_count]) / initial_norm)


def careful(rhs, vol_jac, inv_step, face_jac, orientation):
    selector_np, turning_np = face_tables(Q)
    selector = jnp.asarray(selector_np)
    turning = jnp.asarray(turning_np)
    initial_norm = jnp.sqrt(lax.psum(jnp.sum(rhs * rhs), ("gx", "gy")))
    precond = invert_blocks(vol_jac, inv_step, face_jac, selector)
    orient_hot = (orientation[..., None] == jnp.arange(8, dtype=jnp.int32)).astype(jnp.float32)
    orient_mats = jnp.einsum("...fo,oqp->...fqp", orient_hot, turning, precision=highest)
    krylov_basis = [rhs / initial_norm]
    directions = []
    columns = []
    for iteration in range(ITERS):
        direction = apply_precond(precond, krylov_basis[-1])
        directions.append(direction)
        image_vec = apply_jacobian(direction, vol_jac, inv_step, face_jac, orient_mats, selector)
        column = []
        for vector in krylov_basis:
            projection = lax.psum(jnp.sum(image_vec * vector), ("gx", "gy"))
            image_vec = image_vec - projection * vector
            column.append(projection)
        new_norm = jnp.sqrt(lax.psum(jnp.sum(image_vec * image_vec), ("gx", "gy")))
        column.append(new_norm)
        columns.append(column)
        krylov_basis.append(image_vec / new_norm)
    coefficients, residual_ratio = least_squares(columns, initial_norm)
    update = coefficients[0] * directions[0]
    for index_id in range(1, ITERS):
        update = update + coefficients[index_id] * directions[index_id]
    return (update, residual_ratio)


EL = 4
BLK = NV * NP
LANES = 128
TILES = 3
WIDE = TILES * LANES
GROUPS = BLK // 8
MIN_PIVOT = 0.02
MIN_SCALE = 1e-18
MAX_SCALE = 1e30
DEVICES_AXES = ("gx", "gy")
ROUTE_ORDER = ("far x", "far y", "near y", "near x")


def tile_iota(dim):
    return lax.broadcasted_iota(jnp.int32, (8, LANES), dim)


def turn(x, shift):
    return pltpu.roll(x, shift % 8, 0)


def pick(x, index):
    return jnp.take_along_axis(x, index, axis=1)


def split(x):
    return [x[:, t * LANES : (t + 1) * LANES] for t in range(TILES)]


def face_of_row(pair):
    return 2 * pair + (tile_iota(0) >> 2)


def collect(per_element):
    row = tile_iota(0)
    even = (row & 1) == 0
    low = (row & 2) == 0
    folded = [a + turn(a, 4) for a in per_element]

    def join(mask, first, second, step):
        return jnp.where(mask, first, second) + turn(jnp.where(mask, second, first), -step)

    return join(low, join(even, folded[0], folded[1], 1), join(even, folded[2], folded[3], 1), 2)


def row_masks():
    offset = tile_iota(1) - tile_iota(0)
    return [offset == 8 * k for k in range(LANES // 8)]


def couple_rows(h_ref, y):
    masks = row_masks()
    tiles = [[] for _ in range(TILES)]
    for e in range(EL):
        spread = [jnp.broadcast_to(part[e : e + 1, :], (8, LANES)) for part in y]
        acc = [jnp.zeros((8, LANES), jnp.float32) for _ in range(TILES)]
        for g in range(GROUPS):
            rows = slice(8 * g, 8 * g + 8)
            p = h_ref[e, rows, 0:LANES] * spread[0]
            p = p + h_ref[e, rows, LANES : 2 * LANES] * spread[1]
            p = p + h_ref[e, rows, 2 * LANES : WIDE] * spread[2]
            total = jnp.sum(p, axis=1, keepdims=True)
            t, k = divmod(g, LANES // 8)
            acc[t] = jnp.where(masks[k], total, acc[t])
        for t in range(TILES):
            tiles[t].append(acc[t])
    return [collect(parts) for parts in tiles]


def couple_twice(h_ref, t_ref, y):
    tiles = [[] for _ in range(TILES)]
    for e in range(EL):
        spread = [jnp.broadcast_to(part[e : e + 1, :], (8, LANES)) for part in y]
        acc = [jnp.zeros((8, LANES), jnp.float32) for _ in range(TILES)]
        for g in range(GROUPS):
            rows = slice(8 * g, 8 * g + 8)
            p = h_ref[e, rows, 0:LANES] * spread[0]
            p = p + h_ref[e, rows, LANES : 2 * LANES] * spread[1]
            p = p + h_ref[e, rows, 2 * LANES : WIDE] * spread[2]
            total = jnp.sum(p, axis=1, keepdims=True)
            for t in range(TILES):
                acc[t] = acc[t] + t_ref[e, rows, t * LANES : (t + 1) * LANES] * total
        for t in range(TILES):
            tiles[t].append(acc[t])
    return [collect(parts) for parts in tiles]


def series(h_ref, t_ref, start):
    moved = couple_rows(h_ref, start)
    first = tuple(start[t] + moved[t] for t in range(TILES))

    def step(_, y):
        moved = couple_twice(h_ref, t_ref, y)
        return tuple(first[t] + moved[t] for t in range(TILES))

    return list(lax.fori_loop(0, 2 ** (NS_STEPS - 1) - 1, step, first))


def traces_of(z):
    lane = tile_iota(1)
    var, node = lane >> 4, lane & 15
    s, t = node & 3, node >> 2
    result = []
    for pair in range(3):
        if pair == 0:
            place = 4 * s + 16 * t + 3 * (tile_iota(0) >> 2)
        elif pair == 1:
            place = s + 16 * t + 12 * (tile_iota(0) >> 2)
        else:
            place = s + 4 * t + 48 * (tile_iota(0) >> 2)
        index = (var & 1) * NP + place
        parts = [pick(z[k], index) for k in range(TILES)]
        tile = var >> 1
        result.append(jnp.where(tile == 0, parts[0], jnp.where(tile == 1, parts[1], parts[2])))
    return result


def turned_nodes(code):
    node = tile_iota(1) & 15
    s, t = node & 3, node >> 2
    swap = (code & 4) != 0
    first = jnp.where(swap, t, s)
    second = jnp.where(swap, s, t)
    first = jnp.where((code & 1) != 0, 3 - first, first)
    second = jnp.where((code & 2) != 0, 3 - second, second)
    return first + 4 * second


def through_faces(pair, neighbour, g_ref, q_ref):
    lane = tile_iota(1)
    own = lane >> 4
    turned = q_ref[pair]
    value = None
    for shift in range(NV):
        other = own + shift
        other = jnp.where(other >= NV, other - NV, other)
        index = (other * 16 + turned) & (LANES - 1)
        term = g_ref[3 * shift + pair] * pick(neighbour, index)
        value = term if value is None else value + term
    node = lane & (NP - 1)
    a, b, c = node & 3, (node >> 2) & 3, node >> 4
    end = 3 * (tile_iota(0) >> 2)
    if pair == 0:
        hit, place = a == end, b + 4 * c
    elif pair == 1:
        hit, place = b == end, a + 4 * c
    else:
        hit, place = c == end, a + 4 * b
    lifted = []
    for t in range(TILES):
        index = ((2 * t + (lane >> 6)) * 16 + place) & (LANES - 1)
        keep = hit if t < 2 else hit & (lane < NP)
        lifted.append(jnp.where(keep, pick(value, index), 0.0))
    return lifted


def fold(parts):
    return [p + turn(p, 4) for p in parts]


def across_third(trace):
    row = tile_iota(0)
    inner = jnp.where(row < 4, turn(trace, -3), turn(trace, 3))
    outer = jnp.where(row == 0, turn(trace, 1), turn(trace, -1))
    return jnp.where((row == 0) | (row == 7), outer, inner)


def put(ref, parts):
    for t in range(TILES):
        ref[:, t * LANES : (t + 1) * LANES] = parts[t]


def prepare(vol_ref, rhs_ref, inv_ref, fj_ref, ori_ref, m_ref, d_ref, g_ref, q_ref, r_ref, w_ref, z_ref, tx_ref, ty_ref, tz_ref, held_ref, sems):
    h_ref, t_ref = m_ref.at[0], m_ref.at[1]
    copies = [pltpu.make_async_copy(vol_ref.at[e], held_ref.at[e], sems.at[e]) for e in range(EL)]
    for copy in copies:
        copy.start()
    row, lane = tile_iota(0), tile_iota(1)
    zero = jnp.zeros((8, LANES), jnp.float32)
    r_ref[...] = jnp.zeros((8, WIDE), jnp.float32)
    r_ref[0:4, 0:BLK] = rhs_ref[...]
    r_ref[4:8, 0:BLK] = rhs_ref[...]
    start = split(r_ref[...])
    d_ref[...] = jnp.zeros((8, WIDE), jnp.float32)
    d_ref[0:4, 0:6] = ori_ref[...].astype(jnp.float32)
    d_ref[4:8, 0:6] = ori_ref[...].astype(jnp.float32)
    codes = d_ref[:, 0:LANES]
    for pair in range(3):
        q_ref[pair] = turned_nodes(pick(codes, face_of_row(pair)).astype(jnp.int32))
    packed = []
    for i in range(NV):
        total = zero
        for j in range(NV):
            d_ref[:, 0:LANES] = zero
            d_ref[0:4, 0:6] = fj_ref[i, j]
            d_ref[4:8, 0:6] = fj_ref[i, j]
            part = d_ref[:, 0:LANES]
            total = total + (part if j == 0 else pltpu.roll(part, 16 * j, 1))
        packed.append(total)
    own = lane >> 4
    for shift in range(NV):
        other = own + shift
        other = jnp.where(other >= NV, other - NV, other)
        for pair in range(3):
            index = (other * 16 + face_of_row(pair)) & (LANES - 1)
            value = zero
            for i in range(NV):
                value = jnp.where(own == i, pick(packed[i], index), value)
            if shift == 0:
                value = value - penalty
            g_ref[3 * shift + pair] = jnp.where(own < NV, 0.5 * value, 0.0)
    node = lane & (NP - 1)
    a, b, c = node & 3, (node >> 2) & 3, node >> 4
    cover = [a == 0, a == 3, b == 0, b == 3, c == 0, c == 3]
    node_part = []
    for i in range(NV):
        tiles = []
        for t in range(TILES):
            var = 2 * t + (lane >> 6)
            index = (var * 16) & (LANES - 1)
            value = zero
            for f in range(6):
                term = pick(packed[i], index + f)
                term = term + jnp.where(var == i, penalty, 0.0)
                value = value + jnp.where(cover[f], 0.5 * term, 0.0)
            if t == 2:
                value = jnp.where(lane < NP, value, 0.0)
            tiles.append(value)
        node_part.append(tiles)
    masks = row_masks()
    node_offset = node - row
    inverse = [zero] * TILES
    for e in range(EL):
        copies[e].wait()

        def volume(g, t):
            rows = slice(8 * g, 8 * g + 8)
            if t < 2:
                return held_ref[e, rows, t * LANES : (t + 1) * LANES]
            return jnp.concatenate([held_ref[e, rows, 2 * LANES : BLK], jnp.zeros((8, WIDE - BLK), jnp.float32)], axis=1)

        diag = [zero] * TILES
        for g in range(GROUPS):
            t, k = divmod(g, LANES // 8)
            diag[t] = jnp.where(masks[k], volume(g, t), diag[t])
        scale = []
        for t in range(TILES):
            total = diag[t]
            for step in (4, 2, 1):
                total = total + turn(total, step)
            low, high = node_part[2 * t][t][e : e + 1, :], node_part[min(2 * t + 1, NV - 1)][t][e : e + 1, :]
            own_row = jnp.where(lane[0:1] < NP, low, high) if t < 2 else low
            total = total + jnp.broadcast_to(own_row, (8, LANES)) + inv_ref[e]
            if t == 2:
                total = jnp.where(lane < NP, total, 1.0)
            scale.append(1.0 / total)
            inverse[t] = jnp.where((row & 3) == e, scale[t], inverse[t])
        for i in range(NV):
            spread = [jnp.broadcast_to(node_part[i][t][e : e + 1, :], (8, LANES)) for t in range(TILES)]
            for gi in range(NP // 8):
                g = i * (NP // 8) + gi
                td, k = divmod(g, LANES // 8)
                same_node = node_offset == 8 * gi
                for t in range(TILES):
                    value = volume(g, t) + jnp.where(same_node, spread[t], 0.0)
                    value = -(value * scale[t])
                    if t == td:
                        value = jnp.where(masks[k], 0.0, value)
                    h_ref[e, 8 * g : 8 * g + 8, t * LANES : (t + 1) * LANES] = value
        for bi in range(TILES):
            size = min(LANES, BLK - bi * LANES)
            for bj in range(TILES):
                part = h_ref[e, bi * LANES : bi * LANES + size, bj * LANES : (bj + 1) * LANES]
                if size < LANES:
                    part = jnp.concatenate([part, jnp.zeros((LANES - size, LANES), jnp.float32)], axis=0)
                count = min(LANES, BLK - bj * LANES)
                t_ref[e, bj * LANES : bj * LANES + count, bi * LANES : (bi + 1) * LANES] = part.T[0:count, :]
    put(d_ref, inverse)
    w = series(h_ref, t_ref, start)
    put(w_ref, w)
    z = [inverse[t] * w[t] for t in range(TILES)]
    put(z_ref, z)
    tx_ref[...], ty_ref[...], tz_ref[...] = traces_of(z)


def own_part(m_ref, g_ref, q_ref, r_ref, w_ref, tz_ref, out_ref):
    r, w = split(r_ref[...]), split(w_ref[...])
    moved = couple_rows(m_ref.at[0], w)
    third = fold(through_faces(2, across_third(tz_ref[...]), g_ref, q_ref))
    put(out_ref, [w[t] - moved[t] - r[t] + third[t] for t in range(TILES)])


def arrived(own_axis, pair_ref, far_ref):
    odd = lax.rem(lax.axis_index(own_axis), 2) == 1
    near, far = pair_ref[...], far_ref[...]
    before = jnp.where(odd, near, far)
    after = jnp.where(odd, far, near)
    return turn(jnp.where(tile_iota(0) >= 4, before, after), 4)


def by_route(*refs):
    return [refs[ROUTE_ORDER.index(name)] for name in ("near x", "far x", "near y", "far y")]


def next_vector(part_ref, c_ref, z_ref, x_ref, y_ref, g_ref, q_ref):
    first = through_faces(0, arrived("gx", c_ref, z_ref), g_ref, q_ref)
    second = through_faces(1, arrived("gy", x_ref, y_ref), g_ref, q_ref)
    lifted = fold([first[t] + second[t] for t in range(TILES)])
    part = split(part_ref[...])
    return [part[t] + lifted[t] for t in range(TILES)]


def advance(part_ref, a0_ref, a1_ref, a2_ref, a3_ref, g_ref, q_ref, m_ref, d_ref, r_ref, w_ref, z_ref, tx_ref, ty_ref, tz_ref):
    r = next_vector(part_ref, *by_route(a0_ref, a1_ref, a2_ref, a3_ref), g_ref, q_ref)
    put(r_ref, r)
    w = series(m_ref.at[0], m_ref.at[1], r)
    put(w_ref, w)
    z = [a * b for a, b in zip(split(d_ref[...]), w)]
    put(z_ref, z)
    tx_ref[...], ty_ref[...], tz_ref[...] = traces_of(z)


def products(part_ref, a0_ref, a1_ref, a2_ref, a3_ref, g_ref, q_ref, r0_ref, r1_ref, r2_ref, out_ref):
    last = next_vector(part_ref, *by_route(a0_ref, a1_ref, a2_ref, a3_ref), g_ref, q_ref)
    basis = [split(r0_ref[...]), split(r1_ref[...]), split(r2_ref[...]), last]
    lane = tile_iota(1)
    acc = jnp.zeros((8, LANES), jnp.float32)
    slot = 0
    for i in range(ITERS + 1):
        for j in range(i + 1):
            p = basis[i][0] * basis[j][0] + basis[i][1] * basis[j][1] + basis[i][2] * basis[j][2]
            acc = jnp.where(lane == slot, jnp.sum(p, axis=1, keepdims=True), acc)
            slot += 1
    for step in (1, 2):
        acc = acc + turn(acc, step)
    out_ref[...] = acc


def finish(sums_ref, z1_ref, z2_ref, z3_ref, out_ref, ratio_ref, fine_ref):
    acc = jnp.zeros((8, LANES), jnp.float32)
    parts = [acc] * 4
    for n in range(sums_ref.shape[0] // 8):
        parts[n % 4] = parts[n % 4] + sums_ref[8 * n : 8 * n + 8, :]
    acc = (parts[0] + parts[1]) + (parts[2] + parts[3])
    for step in (1, 2, 4):
        acc = acc + turn(acc, step)
    gram = {}
    slot = 0
    for i in range(ITERS + 1):
        for j in range(i + 1):
            gram[j, i] = pick(acc, jnp.full((8, LANES), slot, jnp.int32))
            slot += 1
    upper = {}
    good = (gram[0, 0] > MIN_SCALE) & (gram[0, 0] < MAX_SCALE)
    for i in range(ITERS + 1):
        pivot = gram[i, i]
        for k in range(i):
            pivot = pivot - upper[k, i] * upper[k, i]
        good = good & (pivot > MIN_PIVOT * gram[i, i]) & (gram[i, i] > MIN_SCALE) & (gram[i, i] < MAX_SCALE)
        upper[i, i] = jnp.sqrt(pivot)
        inverse = 1.0 / upper[i, i]
        for j in range(i + 1, ITERS + 1):
            value = gram[i, j]
            for k in range(i):
                value = value - upper[k, i] * upper[k, j]
            upper[i, j] = value * inverse
    columns = []
    for j in range(1, ITERS + 1):
        column = [upper[i, j] + upper[i, j - 1] for i in range(j)]
        columns.append(column + [upper[j, j]])
    coefficients, ratio = least_squares(columns, upper[0, 0])
    z = [split(z1_ref[...]), split(z2_ref[...]), split(z3_ref[...])]
    for t in range(TILES):
        value = coefficients[0] * z[0][t] + coefficients[1] * z[1][t] + coefficients[2] * z[2][t]
        if t < 2:
            out_ref[:, t * LANES : (t + 1) * LANES] = value[0:EL, :]
        else:
            out_ref[:, 2 * LANES : BLK] = value[0:EL, 0 : BLK - 2 * LANES]
    ratio_ref[0] = ratio[0, 0]
    fine_ref[0] = jnp.where(good, 1, 0)[0, 0]


def shape(*dims, dtype=jnp.float32):
    return jax.ShapeDtypeStruct(dims, dtype)


def call(kernel, outs, args, scalar_args=(), scalar_outs=(), far_args=(), scratch=()):
    in_specs = [
        pl.BlockSpec(memory_space=pltpu.SMEM if n in scalar_args else pl.ANY if n in far_args else pltpu.VMEM)
        for n in range(len(args))
    ]
    single = not isinstance(outs, tuple)
    out_specs = [
        pl.BlockSpec(memory_space=pltpu.SMEM if n in scalar_outs else pltpu.VMEM)
        for n in range(1 if single else len(outs))
    ]
    return pl.pallas_call(
        kernel,
        out_shape=outs,
        in_specs=in_specs,
        out_specs=out_specs[0] if single else tuple(out_specs),
        scratch_shapes=scratch,
        compiler_params=pltpu.CompilerParams(vmem_limit_bytes=16 * 2**20),
    )(*args)


def body(rhs, vol_jac, inv_step, face_jac, orientation):
    nx, ny = lax.axis_size("gx"), lax.axis_size("gy")
    flat = [(x, y) for x in range(nx) for y in range(ny)]

    def pairs(move):
        return [(x * ny + y, (move(x, y)[0] % nx) * ny + move(x, y)[1] % ny) for x, y in flat]

    routes = {
        "near x": pairs(lambda x, y: (x ^ 1, y)),
        "far x": pairs(lambda x, y: (x + 1 if x % 2 else x - 1, y)),
        "near y": pairs(lambda x, y: (x, y ^ 1)),
        "far y": pairs(lambda x, y: (x, y + 1 if y % 2 else y - 1)),
    }

    def exchange(tx, ty):
        return [
            lax.ppermute(tx if name.endswith("x") else ty, DEVICES_AXES, routes[name]) for name in ROUTE_ORDER
        ]

    vec, tr = shape(8, WIDE), shape(8, LANES)
    matrix, inverse, g, q, r0, w, z, tx, ty, tz = call(
        prepare,
        (
            shape(2, EL, BLK, WIDE),
            vec,
            shape(3 * NV, 8, LANES),
            shape(3, 8, LANES, dtype=jnp.int32),
            *[vec] * 3,
            *[tr] * 3,
        ),
        (
            vol_jac.reshape(EL, BLK, BLK),
            rhs.reshape(EL, BLK),
            inv_step.reshape(EL),
            face_jac.reshape(EL, 6, NV, NV).transpose(2, 3, 0, 1),
            orientation.reshape(EL, 6),
        ),
        scalar_args=(2,),
        far_args=(0,),
        scratch=[pltpu.VMEM((EL, BLK, BLK), jnp.float32), pltpu.SemaphoreType.DMA((EL,))],
    )
    basis, directions = [r0], [z]
    for iteration in range(ITERS):
        around = exchange(tx, ty)
        part = call(own_part, vec, (matrix, g, q, basis[-1], w, tz))
        if iteration < ITERS - 1:
            r, w, z, tx, ty, tz = call(
                advance,
                (vec, vec, vec, tr, tr, tr),
                (part, *around, g, q, matrix, inverse),
            )
            basis.append(r)
            directions.append(z)
    total = nx * ny
    sums = call(products, tr, (part, *around, g, q, *basis))
    sums = jnp.broadcast_to(sums[0:1][None], (total, 1, LANES))
    sums = lax.all_to_all(sums, DEVICES_AXES, 0, 0).reshape(total, LANES)
    update, ratio, fine = call(
        finish, (shape(EL, BLK), shape(1), shape(1, dtype=jnp.int32)), (sums, *directions), scalar_outs=(1, 2)
    )
    return lax.cond(
        fine[0] == 1,
        lambda: (update.reshape(rhs.shape), ratio[0]),
        lambda: careful(rhs, vol_jac, inv_step, face_jac, orientation),
    )


def solution(mesh):
    placed = (
        P("gx", "gy", None, None),
        P("gx", "gy", None, None, None),
        P("gx", "gy", None),
        P("gx", "gy", None, None, None, None),
        P("gx", "gy", None, None),
    )
    return jax.shard_map(
        body,
        mesh=mesh,
        in_specs=placed,
        out_specs=(P("gx", "gy", None, None), P()),
        check_vma=False,
    )
```

```python
import jax
import jax.numpy as jnp
import numpy as np
from jax import lax
from jax.experimental import pallas as pl
from jax.experimental.pallas import tpu as pltpu
from jax.sharding import PartitionSpec as P

Q = 4
NV = 5
ITERS = 3
NS_STEPS = 3
NP = 64


penalty = 4.0
highest = lax.Precision.HIGHEST


def extended(shard, sides, width):
    for axis, dim in sides:
        size, length = (lax.axis_size(axis), shard.shape[dim])
        up = [(i, (i + 1) % size) for i in range(size)]
        down = [(j, i) for i, j in up]
        last = lax.slice_in_dim(shard, length - width, length, axis=dim)
        first = lax.slice_in_dim(shard, 0, width, axis=dim)
        before = lax.ppermute(last, axis, up)
        after = lax.ppermute(first, axis, down)
        shard = jnp.concatenate([before, shard, after], axis=dim)
    return shard


def face_tables(nodes_side):
    node_count = nodes_side**3
    across = nodes_side * nodes_side
    selector = np.zeros((6, node_count, across), np.float32)
    for face_id in range(6):
        for node_id in range(node_count):
            first_coord = node_id % nodes_side
            second_coord = node_id // nodes_side % nodes_side
            third_coord = node_id // across
            fixed_axis = [
                first_coord,
                first_coord,
                second_coord,
                second_coord,
                third_coord,
                third_coord,
            ][face_id]
            target = 0 if face_id % 2 == 0 else nodes_side - 1
            if fixed_axis == target:
                plane_pair = [
                    (second_coord, third_coord),
                    (second_coord, third_coord),
                    (first_coord, third_coord),
                    (first_coord, third_coord),
                    (first_coord, second_coord),
                    (first_coord, second_coord),
                ][face_id]
                selector[face_id, node_id, plane_pair[0] + nodes_side * plane_pair[1]] = 1.0
    turning = np.zeros((8, across, across), np.float32)
    for orient_code in range(8):
        for face_node in range(across):
            along_first = face_node % nodes_side
            along_second = face_node // nodes_side
            if orient_code & 4:
                along_first, along_second = (along_second, along_first)
            if orient_code & 1:
                along_first = nodes_side - 1 - along_first
            if orient_code & 2:
                along_second = nodes_side - 1 - along_second
            turning[orient_code, face_node, along_first + nodes_side * along_second] = 1.0
    return (selector, turning)


def element_traces(operand, selector):
    shaped = operand.reshape(operand.shape[:-1] + (NV, NP))
    return jnp.einsum("...vn,fnq->...fvq", shaped, selector, precision=highest)


def lift_faces(face_values, selector):
    lifted = jnp.einsum("...fvq,fnq->...vn", face_values, selector, precision=highest)
    return lifted.reshape(lifted.shape[:-2] + (NV * NP,))


def face_terms(own_traces, oriented, face_jac):
    identity = jnp.eye(NV, dtype=jnp.float32)
    own_part = jnp.einsum(
        "...fij,...fjq->...fiq", face_jac + penalty * identity, own_traces, precision=highest
    )
    other_part = jnp.einsum(
        "...fij,...fjq->...fiq", face_jac - penalty * identity, oriented, precision=highest
    )
    return 0.5 * (own_part + other_part)


def invert_blocks(vol_jac, inv_step, face_jac, selector):
    eye_nodes = jnp.eye(NP, dtype=jnp.float32)
    eye_block = jnp.eye(NV * NP, dtype=jnp.float32)
    coverage = jnp.sum(selector, axis=-1)
    own_face = 0.5 * (face_jac + penalty * jnp.eye(NV, dtype=jnp.float32))
    node_part = jnp.einsum("...fij,fn->...ijn", own_face, coverage, precision=highest)
    face_block = jnp.einsum("...ijn,nm->...injm", node_part, eye_nodes, precision=highest)
    face_block = face_block.reshape(face_block.shape[:-4] + (NV * NP, NV * NP))
    element_block = vol_jac + face_block + inv_step[..., None, None] * eye_block
    diagonal = jnp.diagonal(element_block, axis1=-2, axis2=-1)
    approx = eye_block * (1.0 / diagonal)[..., :, None]
    for sweep_id in range(NS_STEPS):
        product = jnp.einsum("...rk,...kc->...rc", element_block, approx, precision=highest)
        approx = 2.0 * approx - jnp.einsum("...rk,...kc->...rc", approx, product, precision=highest)
    return approx


def apply_precond(precond, operand):
    return jnp.einsum("...rc,...c->...r", precond, operand, precision=highest)


def apply_jacobian(operand, vol_jac, inv_step, face_jac, orient_mats, selector):
    own_traces = element_traces(operand, selector)
    padded = extended(operand, (("gx", 0), ("gy", 1)), 1)
    padded_traces = element_traces(padded, selector)
    side_faces = [
        padded_traces[0:-2, 1:-1, :, 1],
        padded_traces[2:, 1:-1, :, 0],
        padded_traces[1:-1, 0:-2, :, 3],
        padded_traces[1:-1, 2:, :, 2],
    ]
    lower_face = jnp.roll(own_traces, 1, axis=2)[:, :, :, 5]
    upper_face = jnp.roll(own_traces, -1, axis=2)[:, :, :, 4]
    neighbours = jnp.stack(side_faces + [lower_face, upper_face], axis=3)
    oriented = jnp.einsum("...fqp,...fvp->...fvq", orient_mats, neighbours, precision=highest)
    coupled = face_terms(own_traces, oriented, face_jac)
    volume = jnp.einsum("...rc,...c->...r", vol_jac, operand, precision=highest)
    return inv_step[..., None] * operand + volume + lift_faces(coupled, selector)


def least_squares(columns, initial_norm):
    steps_count = len(columns)
    rotations = []
    target_values = [initial_norm] + [jnp.zeros_like(initial_norm)] * steps_count
    upper_rows = []
    for column_id in range(steps_count):
        column = list(columns[column_id])
        for index_id in range(column_id):
            cosine, sine_part = rotations[index_id]
            top_value = cosine * column[index_id] + sine_part * column[index_id + 1]
            column[index_id + 1] = -sine_part * column[index_id] + cosine * column[index_id + 1]
            column[index_id] = top_value
        radius = jnp.sqrt(
            column[column_id] * column[column_id] + column[column_id + 1] * column[column_id + 1]
        )
        cosine = column[column_id] / radius
        sine_part = column[column_id + 1] / radius
        rotations.append((cosine, sine_part))
        column[column_id] = radius
        target_values[column_id + 1] = -sine_part * target_values[column_id]
        target_values[column_id] = cosine * target_values[column_id]
        upper_rows.append(column)
    coefficients = [None] * steps_count
    for row_id in reversed(range(steps_count)):
        running = target_values[row_id]
        for later_id in range(row_id + 1, steps_count):
            running = running - upper_rows[later_id][row_id] * coefficients[later_id]
        coefficients[row_id] = running / upper_rows[row_id][row_id]
    return (coefficients, jnp.abs(target_values[steps_count]) / initial_norm)


def careful(rhs, vol_jac, inv_step, face_jac, orientation):
    selector_np, turning_np = face_tables(Q)
    selector = jnp.asarray(selector_np)
    turning = jnp.asarray(turning_np)
    initial_norm = jnp.sqrt(lax.psum(jnp.sum(rhs * rhs), ("gx", "gy")))
    precond = invert_blocks(vol_jac, inv_step, face_jac, selector)
    orient_hot = (orientation[..., None] == jnp.arange(8, dtype=jnp.int32)).astype(jnp.float32)
    orient_mats = jnp.einsum("...fo,oqp->...fqp", orient_hot, turning, precision=highest)
    krylov_basis = [rhs / initial_norm]
    directions = []
    columns = []
    for iteration in range(ITERS):
        direction = apply_precond(precond, krylov_basis[-1])
        directions.append(direction)
        image_vec = apply_jacobian(direction, vol_jac, inv_step, face_jac, orient_mats, selector)
        column = []
        for vector in krylov_basis:
            projection = lax.psum(jnp.sum(image_vec * vector), ("gx", "gy"))
            image_vec = image_vec - projection * vector
            column.append(projection)
        new_norm = jnp.sqrt(lax.psum(jnp.sum(image_vec * image_vec), ("gx", "gy")))
        column.append(new_norm)
        columns.append(column)
        krylov_basis.append(image_vec / new_norm)
    coefficients, residual_ratio = least_squares(columns, initial_norm)
    update = coefficients[0] * directions[0]
    for index_id in range(1, ITERS):
        update = update + coefficients[index_id] * directions[index_id]
    return (update, residual_ratio)


EL = 4
BLK = NV * NP
LANES = 128
TILES = 3
WIDE = TILES * LANES
GROUPS = BLK // 8
MIN_PIVOT = 0.02
MIN_SCALE = 1e-18
MAX_SCALE = 1e30
DEVICES_AXES = ("gx", "gy")
ROUTE_ORDER = ("near x", "far x", "far y", "near y")


def tile_iota(dim):
    return lax.broadcasted_iota(jnp.int32, (8, LANES), dim)


def turn(x, shift):
    return pltpu.roll(x, shift % 8, 0)


def pick(x, index):
    return jnp.take_along_axis(x, index, axis=1)


def split(x):
    return [x[:, t * LANES : (t + 1) * LANES] for t in range(TILES)]


def face_of_row(pair):
    return 2 * pair + (tile_iota(0) >> 2)


def collect(per_element):
    row = tile_iota(0)
    even = (row & 1) == 0
    low = (row & 2) == 0
    folded = [a + turn(a, 4) for a in per_element]

    def join(mask, first, second, step):
        return jnp.where(mask, first, second) + turn(jnp.where(mask, second, first), -step)

    return join(low, join(even, folded[0], folded[1], 1), join(even, folded[2], folded[3], 1), 2)


def row_masks():
    offset = tile_iota(1) - tile_iota(0)
    return [offset == 8 * k for k in range(LANES // 8)]


def couple_rows(h_ref, y):
    masks = row_masks()
    tiles = [[] for _ in range(TILES)]
    for e in range(EL):
        spread = [jnp.broadcast_to(part[e : e + 1, :], (8, LANES)) for part in y]
        acc = [jnp.zeros((8, LANES), jnp.float32) for _ in range(TILES)]
        for g in range(GROUPS):
            rows = slice(8 * g, 8 * g + 8)
            p = h_ref[e, rows, 0:LANES] * spread[0]
            p = p + h_ref[e, rows, LANES : 2 * LANES] * spread[1]
            p = p + h_ref[e, rows, 2 * LANES : WIDE] * spread[2]
            total = jnp.sum(p, axis=1, keepdims=True)
            t, k = divmod(g, LANES // 8)
            acc[t] = jnp.where(masks[k], total, acc[t])
        for t in range(TILES):
            tiles[t].append(acc[t])
    return [collect(parts) for parts in tiles]


def couple_twice(h_ref, t_ref, y):
    tiles = [[] for _ in range(TILES)]
    for e in range(EL):
        spread = [jnp.broadcast_to(part[e : e + 1, :], (8, LANES)) for part in y]
        acc = [jnp.zeros((8, LANES), jnp.float32) for _ in range(TILES)]
        for g in range(GROUPS):
            rows = slice(8 * g, 8 * g + 8)
            p = h_ref[e, rows, 0:LANES] * spread[0]
            p = p + h_ref[e, rows, LANES : 2 * LANES] * spread[1]
            p = p + h_ref[e, rows, 2 * LANES : WIDE] * spread[2]
            total = jnp.sum(p, axis=1, keepdims=True)
            for t in range(TILES):
                acc[t] = acc[t] + t_ref[e, rows, t * LANES : (t + 1) * LANES] * total
        for t in range(TILES):
            tiles[t].append(acc[t])
    return [collect(parts) for parts in tiles]


def series(h_ref, t_ref, start):
    moved = couple_rows(h_ref, start)
    first = tuple(start[t] + moved[t] for t in range(TILES))

    def step(_, y):
        moved = couple_twice(h_ref, t_ref, y)
        return tuple(first[t] + moved[t] for t in range(TILES))

    return list(lax.fori_loop(0, 2 ** (NS_STEPS - 1) - 1, step, first))


def traces_of(z):
    lane = tile_iota(1)
    var, node = lane >> 4, lane & 15
    s, t = node & 3, node >> 2
    result = []
    for pair in range(3):
        if pair == 0:
            place = 4 * s + 16 * t + 3 * (tile_iota(0) >> 2)
        elif pair == 1:
            place = s + 16 * t + 12 * (tile_iota(0) >> 2)
        else:
            place = s + 4 * t + 48 * (tile_iota(0) >> 2)
        index = (var & 1) * NP + place
        parts = [pick(z[k], index) for k in range(TILES)]
        tile = var >> 1
        result.append(jnp.where(tile == 0, parts[0], jnp.where(tile == 1, parts[1], parts[2])))
    return result


def turned_nodes(code):
    node = tile_iota(1) & 15
    s, t = node & 3, node >> 2
    swap = (code & 4) != 0
    first = jnp.where(swap, t, s)
    second = jnp.where(swap, s, t)
    first = jnp.where((code & 1) != 0, 3 - first, first)
    second = jnp.where((code & 2) != 0, 3 - second, second)
    return first + 4 * second


def through_faces(pair, neighbour, g_ref, q_ref):
    lane = tile_iota(1)
    own = lane >> 4
    turned = q_ref[pair]
    value = None
    for shift in range(NV):
        other = own + shift
        other = jnp.where(other >= NV, other - NV, other)
        index = (other * 16 + turned) & (LANES - 1)
        term = g_ref[3 * shift + pair] * pick(neighbour, index)
        value = term if value is None else value + term
    node = lane & (NP - 1)
    a, b, c = node & 3, (node >> 2) & 3, node >> 4
    end = 3 * (tile_iota(0) >> 2)
    if pair == 0:
        hit, place = a == end, b + 4 * c
    elif pair == 1:
        hit, place = b == end, a + 4 * c
    else:
        hit, place = c == end, a + 4 * b
    lifted = []
    for t in range(TILES):
        index = ((2 * t + (lane >> 6)) * 16 + place) & (LANES - 1)
        keep = hit if t < 2 else hit & (lane < NP)
        lifted.append(jnp.where(keep, pick(value, index), 0.0))
    return lifted


def fold(parts):
    return [p + turn(p, 4) for p in parts]


def across_third(trace):
    row = tile_iota(0)
    inner = jnp.where(row < 4, turn(trace, -3), turn(trace, 3))
    outer = jnp.where(row == 0, turn(trace, 1), turn(trace, -1))
    return jnp.where((row == 0) | (row == 7), outer, inner)


def put(ref, parts):
    for t in range(TILES):
        ref[:, t * LANES : (t + 1) * LANES] = parts[t]


def prepare(vol_ref, rhs_ref, inv_ref, fj_ref, ori_ref, m_ref, d_ref, g_ref, q_ref, r_ref, w_ref, z_ref, tx_ref, ty_ref, tz_ref, held_ref, sems):
    h_ref, t_ref = m_ref.at[0], m_ref.at[1]
    copies = [pltpu.make_async_copy(vol_ref.at[e], held_ref.at[e], sems.at[e]) for e in range(EL)]
    for copy in copies:
        copy.start()
    row, lane = tile_iota(0), tile_iota(1)
    zero = jnp.zeros((8, LANES), jnp.float32)
    r_ref[...] = jnp.zeros((8, WIDE), jnp.float32)
    r_ref[0:4, 0:BLK] = rhs_ref[...]
    r_ref[4:8, 0:BLK] = rhs_ref[...]
    start = split(r_ref[...])
    d_ref[...] = jnp.zeros((8, WIDE), jnp.float32)
    d_ref[0:4, 0:6] = ori_ref[...].astype(jnp.float32)
    d_ref[4:8, 0:6] = ori_ref[...].astype(jnp.float32)
    codes = d_ref[:, 0:LANES]
    for pair in range(3):
        q_ref[pair] = turned_nodes(pick(codes, face_of_row(pair)).astype(jnp.int32))
    packed = []
    for i in range(NV):
        total = zero
        for j in range(NV):
            d_ref[:, 0:LANES] = zero
            d_ref[0:4, 0:6] = fj_ref[i, j]
            d_ref[4:8, 0:6] = fj_ref[i, j]
            part = d_ref[:, 0:LANES]
            total = total + (part if j == 0 else pltpu.roll(part, 16 * j, 1))
        packed.append(total)
    own = lane >> 4
    for shift in range(NV):
        other = own + shift
        other = jnp.where(other >= NV, other - NV, other)
        for pair in range(3):
            index = (other * 16 + face_of_row(pair)) & (LANES - 1)
            value = zero
            for i in range(NV):
                value = jnp.where(own == i, pick(packed[i], index), value)
            if shift == 0:
                value = value - penalty
            g_ref[3 * shift + pair] = jnp.where(own < NV, 0.5 * value, 0.0)
    node = lane & (NP - 1)
    a, b, c = node & 3, (node >> 2) & 3, node >> 4
    cover = [a == 0, a == 3, b == 0, b == 3, c == 0, c == 3]
    node_part = []
    for i in range(NV):
        tiles = []
        for t in range(TILES):
            var = 2 * t + (lane >> 6)
            index = (var * 16) & (LANES - 1)
            value = zero
            for f in range(6):
                term = pick(packed[i], index + f)
                term = term + jnp.where(var == i, penalty, 0.0)
                value = value + jnp.where(cover[f], 0.5 * term, 0.0)
            if t == 2:
                value = jnp.where(lane < NP, value, 0.0)
            tiles.append(value)
        node_part.append(tiles)
    masks = row_masks()
    node_offset = node - row
    inverse = [zero] * TILES
    for e in range(EL):
        copies[e].wait()

        def volume(g, t):
            rows = slice(8 * g, 8 * g + 8)
            if t < 2:
                return held_ref[e, rows, t * LANES : (t + 1) * LANES]
            return jnp.concatenate([held_ref[e, rows, 2 * LANES : BLK], jnp.zeros((8, WIDE - BLK), jnp.float32)], axis=1)

        diag = [zero] * TILES
        for g in range(GROUPS):
            t, k = divmod(g, LANES // 8)
            diag[t] = jnp.where(masks[k], volume(g, t), diag[t])
        scale = []
        for t in range(TILES):
            total = diag[t]
            for step in (4, 2, 1):
                total = total + turn(total, step)
            low, high = node_part[2 * t][t][e : e + 1, :], node_part[min(2 * t + 1, NV - 1)][t][e : e + 1, :]
            own_row = jnp.where(lane[0:1] < NP, low, high) if t < 2 else low
            total = total + jnp.broadcast_to(own_row, (8, LANES)) + inv_ref[e]
            if t == 2:
                total = jnp.where(lane < NP, total, 1.0)
            scale.append(1.0 / total)
            inverse[t] = jnp.where((row & 3) == e, scale[t], inverse[t])
        for i in range(NV):
            spread = [jnp.broadcast_to(node_part[i][t][e : e + 1, :], (8, LANES)) for t in range(TILES)]
            for gi in range(NP // 8):
                g = i * (NP // 8) + gi
                td, k = divmod(g, LANES // 8)
                same_node = node_offset == 8 * gi
                for t in range(TILES):
                    value = volume(g, t) + jnp.where(same_node, spread[t], 0.0)
                    value = -(value * scale[t])
                    if t == td:
                        value = jnp.where(masks[k], 0.0, value)
                    h_ref[e, 8 * g : 8 * g + 8, t * LANES : (t + 1) * LANES] = value
        for bi in range(TILES):
            size = min(LANES, BLK - bi * LANES)
            for bj in range(TILES):
                part = h_ref[e, bi * LANES : bi * LANES + size, bj * LANES : (bj + 1) * LANES]
                if size < LANES:
                    part = jnp.concatenate([part, jnp.zeros((LANES - size, LANES), jnp.float32)], axis=0)
                count = min(LANES, BLK - bj * LANES)
                t_ref[e, bj * LANES : bj * LANES + count, bi * LANES : (bi + 1) * LANES] = part.T[0:count, :]
    put(d_ref, inverse)
    w = series(h_ref, t_ref, start)
    put(w_ref, w)
    z = [inverse[t] * w[t] for t in range(TILES)]
    put(z_ref, z)
    tx_ref[...], ty_ref[...], tz_ref[...] = traces_of(z)


def own_part(m_ref, g_ref, q_ref, r_ref, w_ref, tz_ref, out_ref):
    r, w = split(r_ref[...]), split(w_ref[...])
    moved = couple_rows(m_ref.at[0], w)
    third = fold(through_faces(2, across_third(tz_ref[...]), g_ref, q_ref))
    put(out_ref, [w[t] - moved[t] - r[t] + third[t] for t in range(TILES)])


def arrived(own_axis, pair_ref, far_ref):
    odd = lax.rem(lax.axis_index(own_axis), 2) == 1
    near, far = pair_ref[...], far_ref[...]
    before = jnp.where(odd, near, far)
    after = jnp.where(odd, far, near)
    return turn(jnp.where(tile_iota(0) >= 4, before, after), 4)


def by_route(*refs):
    return [refs[ROUTE_ORDER.index(name)] for name in ("near x", "far x", "near y", "far y")]


def next_vector(part_ref, c_ref, z_ref, x_ref, y_ref, g_ref, q_ref):
    first = through_faces(0, arrived("gx", c_ref, z_ref), g_ref, q_ref)
    second = through_faces(1, arrived("gy", x_ref, y_ref), g_ref, q_ref)
    lifted = fold([first[t] + second[t] for t in range(TILES)])
    part = split(part_ref[...])
    return [part[t] + lifted[t] for t in range(TILES)]


def advance(part_ref, a0_ref, a1_ref, a2_ref, a3_ref, g_ref, q_ref, m_ref, d_ref, r_ref, w_ref, z_ref, tx_ref, ty_ref, tz_ref):
    r = next_vector(part_ref, *by_route(a0_ref, a1_ref, a2_ref, a3_ref), g_ref, q_ref)
    put(r_ref, r)
    w = series(m_ref.at[0], m_ref.at[1], r)
    put(w_ref, w)
    z = [a * b for a, b in zip(split(d_ref[...]), w)]
    put(z_ref, z)
    tx_ref[...], ty_ref[...], tz_ref[...] = traces_of(z)


def products(part_ref, a0_ref, a1_ref, a2_ref, a3_ref, g_ref, q_ref, r0_ref, r1_ref, r2_ref, out_ref):
    last = next_vector(part_ref, *by_route(a0_ref, a1_ref, a2_ref, a3_ref), g_ref, q_ref)
    basis = [split(r0_ref[...]), split(r1_ref[...]), split(r2_ref[...]), last]
    lane = tile_iota(1)
    acc = jnp.zeros((8, LANES), jnp.float32)
    slot = 0
    for i in range(ITERS + 1):
        for j in range(i + 1):
            p = basis[i][0] * basis[j][0] + basis[i][1] * basis[j][1] + basis[i][2] * basis[j][2]
            acc = jnp.where(lane == slot, jnp.sum(p, axis=1, keepdims=True), acc)
            slot += 1
    for step in (1, 2):
        acc = acc + turn(acc, step)
    out_ref[...] = acc


def finish(sums_ref, z1_ref, z2_ref, z3_ref, out_ref, ratio_ref, fine_ref):
    acc = jnp.zeros((8, LANES), jnp.float32)
    parts = [acc] * 4
    for n in range(sums_ref.shape[0] // 8):
        parts[n % 4] = parts[n % 4] + sums_ref[8 * n : 8 * n + 8, :]
    acc = (parts[0] + parts[1]) + (parts[2] + parts[3])
    for step in (1, 2, 4):
        acc = acc + turn(acc, step)
    gram = {}
    slot = 0
    for i in range(ITERS + 1):
        for j in range(i + 1):
            gram[j, i] = pick(acc, jnp.full((8, LANES), slot, jnp.int32))
            slot += 1
    upper = {}
    good = (gram[0, 0] > MIN_SCALE) & (gram[0, 0] < MAX_SCALE)
    for i in range(ITERS + 1):
        pivot = gram[i, i]
        for k in range(i):
            pivot = pivot - upper[k, i] * upper[k, i]
        good = good & (pivot > MIN_PIVOT * gram[i, i]) & (gram[i, i] > MIN_SCALE) & (gram[i, i] < MAX_SCALE)
        upper[i, i] = jnp.sqrt(pivot)
        inverse = 1.0 / upper[i, i]
        for j in range(i + 1, ITERS + 1):
            value = gram[i, j]
            for k in range(i):
                value = value - upper[k, i] * upper[k, j]
            upper[i, j] = value * inverse
    columns = []
    for j in range(1, ITERS + 1):
        column = [upper[i, j] + upper[i, j - 1] for i in range(j)]
        columns.append(column + [upper[j, j]])
    coefficients, ratio = least_squares(columns, upper[0, 0])
    z = [split(z1_ref[...]), split(z2_ref[...]), split(z3_ref[...])]
    for t in range(TILES):
        value = coefficients[0] * z[0][t] + coefficients[1] * z[1][t] + coefficients[2] * z[2][t]
        if t < 2:
            out_ref[:, t * LANES : (t + 1) * LANES] = value[0:EL, :]
        else:
            out_ref[:, 2 * LANES : BLK] = value[0:EL, 0 : BLK - 2 * LANES]
    ratio_ref[0] = ratio[0, 0]
    fine_ref[0] = jnp.where(good, 1, 0)[0, 0]


def shape(*dims, dtype=jnp.float32):
    return jax.ShapeDtypeStruct(dims, dtype)


def call(kernel, outs, args, scalar_args=(), scalar_outs=(), far_args=(), scratch=()):
    in_specs = [
        pl.BlockSpec(memory_space=pltpu.SMEM if n in scalar_args else pl.ANY if n in far_args else pltpu.VMEM)
        for n in range(len(args))
    ]
    single = not isinstance(outs, tuple)
    out_specs = [
        pl.BlockSpec(memory_space=pltpu.SMEM if n in scalar_outs else pltpu.VMEM)
        for n in range(1 if single else len(outs))
    ]
    return pl.pallas_call(
        kernel,
        out_shape=outs,
        in_specs=in_specs,
        out_specs=out_specs[0] if single else tuple(out_specs),
        scratch_shapes=scratch,
        compiler_params=pltpu.CompilerParams(vmem_limit_bytes=16 * 2**20),
    )(*args)


def body(rhs, vol_jac, inv_step, face_jac, orientation):
    nx, ny = lax.axis_size("gx"), lax.axis_size("gy")
    flat = [(x, y) for x in range(nx) for y in range(ny)]

    def pairs(move):
        return [(x * ny + y, (move(x, y)[0] % nx) * ny + move(x, y)[1] % ny) for x, y in flat]

    routes = {
        "near x": pairs(lambda x, y: (x ^ 1, y)),
        "far x": pairs(lambda x, y: (x + 1 if x % 2 else x - 1, y)),
        "near y": pairs(lambda x, y: (x, y ^ 1)),
        "far y": pairs(lambda x, y: (x, y + 1 if y % 2 else y - 1)),
    }

    def exchange(tx, ty):
        return [
            lax.ppermute(tx if name.endswith("x") else ty, DEVICES_AXES, routes[name]) for name in ROUTE_ORDER
        ]

    vec, tr = shape(8, WIDE), shape(8, LANES)
    matrix, inverse, g, q, r0, w, z, tx, ty, tz = call(
        prepare,
        (
            shape(2, EL, BLK, WIDE),
            vec,
            shape(3 * NV, 8, LANES),
            shape(3, 8, LANES, dtype=jnp.int32),
            *[vec] * 3,
            *[tr] * 3,
        ),
        (
            vol_jac.reshape(EL, BLK, BLK),
            rhs.reshape(EL, BLK),
            inv_step.reshape(EL),
            face_jac.reshape(EL, 6, NV, NV).transpose(2, 3, 0, 1),
            orientation.reshape(EL, 6),
        ),
        scalar_args=(2,),
        far_args=(0,),
        scratch=[pltpu.VMEM((EL, BLK, BLK), jnp.float32), pltpu.SemaphoreType.DMA((EL,))],
    )
    basis, directions = [r0], [z]
    for iteration in range(ITERS):
        around = exchange(tx, ty)
        part = call(own_part, vec, (matrix, g, q, basis[-1], w, tz))
        if iteration < ITERS - 1:
            r, w, z, tx, ty, tz = call(
                advance,
                (vec, vec, vec, tr, tr, tr),
                (part, *around, g, q, matrix, inverse),
            )
            basis.append(r)
            directions.append(z)
    total = nx * ny
    sums = call(products, tr, (part, *around, g, q, *basis))
    sums = jnp.broadcast_to(sums[0:1][None], (total, 1, LANES))
    sums = lax.all_to_all(sums, DEVICES_AXES, 0, 0).reshape(total, LANES)
    update, ratio, fine = call(
        finish, (shape(EL, BLK), shape(1), shape(1, dtype=jnp.int32)), (sums, *directions), scalar_outs=(1, 2)
    )
    return lax.cond(
        fine[0] == 1,
        lambda: (update.reshape(rhs.shape), ratio[0]),
        lambda: careful(rhs, vol_jac, inv_step, face_jac, orientation),
    )


def solution(mesh):
    placed = (
        P("gx", "gy", None, None),
        P("gx", "gy", None, None, None),
        P("gx", "gy", None),
        P("gx", "gy", None, None, None, None),
        P("gx", "gy", None, None),
    )
    return jax.shard_map(
        body,
        mesh=mesh,
        in_specs=placed,
        out_specs=(P("gx", "gy", None, None), P()),
        check_vma=False,
    )
```
